512 devices in a mesh: inst: 8 (over y_hi, x), space: 64 (over y_lo, z, core).
Axes of the slice: x: 4, y: 4 (y_hi: 2, y_lo: 2; y = y_hi * 2 + y_lo), z: 16, core: 2. Of those that a mesh axis runs over, the one named last changes fastest.
Arguments:
- state: float32 [8, 6, 1024, 2048], P('inst', None, 'space'), may hold values from -6 to 6
- radius: float32 [1024, 2048], P('space'), may hold values from 0.5 to 4
- mixing: float32 [6, 6], replicated, may hold values from -2.5 to 2.5
- donor: int32 [8, 256, 2], P('inst', 'space'), may hold values from 0 to 127, as said below
- intersection: float32 [8, 256], P('inst', 'space'), may hold values from 0 to 1
Outputs:
- updated: float32 [8, 6, 1024, 2048], P('inst', None, 'space')
The draws below stay inside these ranges and needn't reach their ends.
Inputs may be any that keep to these rules, and one draw needn't show every extreme that they name: For each instance n, donor[n, s, 0] is (s * 128) // 256 + (n * 128) // 8 - 2 plus one number of 0 to 1 common to all s of that instance plus 0 or 1, modulo 128; donor[n, s, 1] is donor[n, s, 0] + 1 modulo 128.
All inputs are finite; a program needn't handle non-finite values.
Results may differ from the reference program's by a relative error of at most 0.0003.
Values sent between devices are 32-bit elements; how exact they have to be, the bound alone decides.
No kernel may reach another device: no remote copies, remote signals or barrier semaphores. Data moves between devices by JAX's collectives and lax.ppermute only.
A program may use at most 64 MiB of HBM per device.

```python
import math
import jax
import jax.numpy as jnp
from jax import lax

NV = 6
CX = 16
CW = 2048
RS = 2
RI = 4
NT = 8
NX = 1024
SLOTS = 256
DONORS = 128


def draw_donor(key, part):
    key_offset = jax.random.fold_in(key, 11)
    key_jitter = jax.random.fold_in(key, 23)
    shift_one = jax.random.randint(key_offset, (NT, 1), 0, RS, dtype=jnp.int32)
    slide = jnp.arange(NT, dtype=jnp.int32)[:, None] * DONORS // NT - RS
    jitter = jax.random.randint(key_jitter, (NT, SLOTS), 0, 2, dtype=jnp.int32)
    base = jnp.arange(SLOTS, dtype=jnp.int32) * DONORS // SLOTS
    first = (base[None, :] + slide + shift_one + jitter) % DONORS
    second = (first + 1) % DONORS
    return jnp.stack([first, second], axis=-1).astype(jnp.int32)


def block_scale(stream_key, extent, shards, low, high):
    factor_of = 1.0
    for axis_at, parts in shards:
        heights = jax.random.uniform(jax.random.fold_in(jax.random.fold_in(stream_key, 6), axis_at), (parts,), jnp.float32, low / len(shards), high / len(shards))
        factor_of = factor_of * jnp.repeat(jnp.exp(heights), extent[axis_at] // parts).reshape((-1,) + (1,) * (len(extent) - 1 - axis_at))
    return factor_of


def bell_draw(rng, extent, deviation, bound, cuts=(), kind=jnp.bfloat16):
    gain = block_scale(rng, extent, cuts, -0.22, 0.18) if cuts else 1.0
    drawn = jax.random.normal(rng, extent, jnp.float32) * deviation * gain
    return jnp.minimum(jnp.maximum(drawn, -bound), bound).astype(kind)


def setup_inputs(seed: int = 0) -> dict:
    arg_keys = jax.random.split(jax.random.key(seed), 6)
    state = bell_draw(arg_keys[0], (NT, NV, NX, CW), 1.0, 6.0, ((0, 8), (2, 64)), jnp.float32)
    radius = jnp.clip(jnp.exp(math.log(4.0) - 2.0794415 * jax.random.uniform(arg_keys[1], (NX, CW), jnp.float32) ** block_scale(arg_keys[1], (NX, CW), ((0, 64),), -0.2, 0.2)), 0.5, 4.0)
    mixing = bell_draw(arg_keys[2], (NV, NV), NV ** -0.5, 2.5, (), jnp.float32)
    donor = draw_donor(jax.random.fold_in(arg_keys[5], 71), 0)
    intersection = jnp.clip(1.0 * jax.random.uniform(arg_keys[4], (NT, SLOTS), jnp.float32) ** block_scale(arg_keys[4], (NT, SLOTS), ((0, 8), (1, 64)), -0.2, 0.2), 0.0, 1.0)
    return dict(state=state, radius=radius, mixing=mixing, donor=donor, intersection=intersection)


def spectral_matrix(count):
    rows = jnp.arange(count, dtype=jnp.int32)
    offset = (rows[:, None] - rows[None, :]) % count
    angle = jnp.pi * offset.astype(jnp.float32) / count
    sign = (1 - 2 * (offset % 2)).astype(jnp.float32)
    safe_sin = jnp.where(offset == 0, jnp.float32(1.0), jnp.sin(angle))
    first_part = jnp.where(offset == 0, jnp.float32(0.0), 0.5 * sign * jnp.cos(angle) / safe_sin)
    diag_value = -(jnp.float32(count * count) + 2.0) / 12.0
    second_part = jnp.where(offset == 0, diag_value, -sign / (2.0 * safe_sin * safe_sin))
    return first_part + 0.25 * second_part


def residual_one(field, mixing, donor_one, intersection_one):
    padded = jnp.pad(field, ((0, 0), (1, 1), (1, 1)))
    below = padded[:, :-2, 1:-1]
    above = padded[:, 2:, 1:-1]
    left = padded[:, 1:-1, :-2]
    right = padded[:, 1:-1, 2:]
    flux = 1.0 * (field - below) + 0.5 * (field - left)
    flux = flux + 0.25 * (4.0 * field - below - above - left - right)
    flux = flux + jnp.einsum("vu,uxw->vxw", mixing, field, precision=lax.Precision.HIGHEST)
    slots = jnp.arange(SLOTS, dtype=jnp.int32)
    target_rows = (slots // RI) * CX + slots % RI
    first = donor_one[:, 0]
    second = donor_one[:, 1]
    first_rows = (first // RS) * CX + CX - RS + first % RS
    second_rows = (second // RS) * CX + CX - RS + second % RS
    ghost = intersection_one[None, :, None] * field[:, first_rows, :] + (1.0 - intersection_one)[None, :, None] * field[:, second_rows, :]
    penalty = 2.0 * (field[:, target_rows, :] - ghost)
    return flux.at[:, target_rows, :].add(penalty)


def reference(state, radius, mixing, donor, intersection):
    dmat = spectral_matrix(NT)

    def one_instance(index):
        field = state[index]
        resid = residual_one(field, mixing, donor[index], intersection[index])
        spectral = jnp.tensordot(dmat[index], state, axes=1, precision=lax.Precision.HIGHEST)
        return field - (0.5 / radius)[None] * (resid + spectral)

    return lax.map(one_instance, jnp.arange(NT, dtype=jnp.int32))
```

```python
import math

import jax
import jax.numpy as jnp
from jax import lax
from jax.experimental import pallas as pl
from jax.experimental.pallas import tpu as pltpu
from jax.sharding import PartitionSpec as P

NV = 6
CX = 16
CW = 2048
RI = 4
NT = 8
SPACE = 64
DONORS = 128
LANES = 128
TILES_W = CW // LANES
CHUNK = NV * CX * CW // (8 * LANES) // NT


def spectral_weights():
    out = []
    for k in range(NT):
        if k == 0:
            out.append(0.25 * (-(NT * NT + 2.0) / 12.0))
        else:
            sign = 1.0 - 2.0 * (k % 2)
            angle = math.pi * k / NT
            out.append(
                0.5 * sign * math.cos(angle) / math.sin(angle)
                + 0.25 * (-sign / (2.0 * math.sin(angle) ** 2))
            )
    return out


WEIGHTS = spectral_weights()


def spectral_kernel(x_ref, o_ref):
    def body(t, carry):
        xs = [x_ref[m, t] for m in range(NT)]
        for n in range(NT):
            total = WEIGHTS[0] * xs[n]
            for k in range(1, NT):
                total = total + WEIGHTS[k] * xs[(n - k) % NT]
            o_ref[n, t] = total
        return carry

    lax.fori_loop(0, CHUNK, body, 0, unroll=2)


def update_kernel(
    mixing_ref, donor_ref, inter_ref, state_ref, radius_ref, up_ref, down_ref, ghost_ref,
    spec_ref, out_ref,
):
    p = lax.axis_index("space")
    n = lax.axis_index("inst")
    row = lax.broadcasted_iota(jnp.int32, (8, LANES), 0)
    lane = lax.broadcasted_iota(jnp.int32, (8, LANES), 1)
    base = 2 * (p + 8 * n - 1)
    table = [jnp.zeros((8, LANES), jnp.float32) for _ in range(5)]
    for j in range(RI):
        w = inter_ref[0, j]
        first = (donor_ref[0, j, 0] - base + 2 * DONORS) % DONORS
        second = (donor_ref[0, j, 1] - base + 2 * DONORS) % DONORS
        for r in range(5):
            here = jnp.where(first == r, w, 0.0) + jnp.where(second == r, 1.0 - w, 0.0)
            table[r] = jnp.where(row == j, 2.0 * here, table[r])
    extra = jnp.where(row < RI, 2.0, 0.0)
    lo = jnp.where(p == 0, 0.0, 1.25)
    hi = jnp.where(p == SPACE - 1, 0.0, 0.25)
    mix = [[mixing_ref[v, u] for u in range(NV)] for v in range(NV)]

    def body(c, carry):
        at = pl.multiple_of(c * LANES, LANES)
        left = pl.multiple_of(jnp.maximum(c - 1, 0) * LANES, LANES)
        right = pl.multiple_of(jnp.minimum(c + 1, TILES_W - 1) * LANES, LANES)
        cols = pl.ds(at, LANES)
        wl = jnp.where(jnp.logical_and(c == 0, lane == 0), 0.0, 0.75)
        wr = jnp.where(jnp.logical_and(c == TILES_W - 1, lane == LANES - 1), 0.0, 0.25)
        scale = [0.5 / radius_ref[8 * h : 8 * h + 8, cols] for h in range(2)]
        cur = [[state_ref[0, v, 8 * h : 8 * h + 8, cols] for h in range(2)] for v in range(NV)]
        for v in range(NV):
            before = up_ref[v, 1:2, cols] * lo
            after = down_ref[v, 0:1, cols] * hi
            c0, c1 = cur[v]
            xm = [
                jnp.where(row == 0, before, 1.25 * pltpu.roll(c0, 1, 0)),
                1.25 * pltpu.roll(jnp.where(row == 7, c0, c1), 1, 0),
            ]
            xp = [
                0.25 * pltpu.roll(jnp.where(row == 0, c1, c0), 7, 0),
                jnp.where(row == 7, after, 0.25 * pltpu.roll(c1, 7, 0)),
            ]
            for h in range(2):
                mine = cur[v][h]
                prev = state_ref[0, v, 8 * h : 8 * h + 8, pl.ds(left, LANES)]
                nxt = state_ref[0, v, 8 * h : 8 * h + 8, pl.ds(right, LANES)]
                wm = pltpu.roll(jnp.where(lane == LANES - 1, prev, mine), 1, 1)
                wp = pltpu.roll(jnp.where(lane == 0, nxt, mine), LANES - 1, 1)
                total = 2.5 * mine - xm[h] - xp[h] - wl * wm - wr * wp
                for u in range(NV):
                    total = total + mix[v][u] * cur[u][h]
                if h == 0:
                    total = total + extra * mine
                    for r in range(5):
                        total = total - table[r] * ghost_ref[v, r : r + 1, cols]
                total = total + spec_ref[(v * 2 + h) * TILES_W + c]
                out_ref[0, v, 8 * h : 8 * h + 8, cols] = mine - scale[h] * total
        return carry

    lax.fori_loop(0, TILES_W, body, 0)


def on_device(state, radius, mixing, donor, intersection):
    field = state[0]
    tiles = field.reshape(NV, 2, 8, TILES_W, LANES).transpose(0, 1, 3, 2, 4).reshape(-1, 8, LANES)
    spread = lax.all_to_all(tiles, "inst", 0, 0, tiled=True)

    up = lax.ppermute(field[:, CX - 2 :], "space", [(i, (i + 1) % SPACE) for i in range(SPACE)])
    edge = jnp.concatenate([field[:, :1], field[:, CX - 2 : CX - 1]], axis=1)
    down = lax.ppermute(edge, "space", [((i + 1) % SPACE, i) for i in range(SPACE)])
    donors = jnp.concatenate([up, field[:, CX - 2 :], down[:, 1:]], axis=1)
    moves = [
        (n * SPACE + (p + 8 * n) % SPACE, n * SPACE + p) for n in range(NT) for p in range(SPACE)
    ]
    ghost = lax.ppermute(donors, ("inst", "space"), moves)

    mixed = pl.pallas_call(
        spectral_kernel,
        out_shape=jax.ShapeDtypeStruct((NT, CHUNK, 8, LANES), jnp.float32),
        name="spectral",
    )(spread.reshape(NT, CHUNK, 8, LANES))
    spec = lax.all_to_all(mixed.reshape(-1, 8, LANES), "inst", 0, 0, tiled=True)

    vmem = pl.BlockSpec(memory_space=pltpu.VMEM)
    smem = pl.BlockSpec(memory_space=pltpu.SMEM)
    return pl.pallas_call(
        update_kernel,
        out_shape=jax.ShapeDtypeStruct(state.shape, jnp.float32),
        in_specs=[smem, smem, smem] + [vmem] * 6,
        out_specs=vmem,
        name="update",
    )(mixing, donor, intersection, state, radius, up, down, ghost, spec)


def solution(mesh):
    in_specs = (
        P("inst", None, "space", None),
        P("space", None),
        P(),
        P("inst", "space", None),
        P("inst", "space"),
    )
    out_specs = P("inst", None, "space", None)
    return jax.shard_map(
        on_device, mesh=mesh, in_specs=in_specs, out_specs=out_specs, check_vma=False
    )
```

```python
import math

import jax
import jax.numpy as jnp
from jax import lax
from jax.experimental import pallas as pl
from jax.experimental.pallas import tpu as pltpu
from jax.sharding import PartitionSpec as P

NV = 6
CX = 16
CW = 2048
RI = 4
NT = 8
SPACE = 64
DONORS = 128
LANES = 128
TILES_W = CW // LANES
CHUNK = NV * CX * CW // (8 * LANES) // NT


def spectral_weights():
    out = []
    for k in range(NT):
        if k == 0:
            out.append(0.25 * (-(NT * NT + 2.0) / 12.0))
        else:
            sign = 1.0 - 2.0 * (k % 2)
            angle = math.pi * k / NT
            out.append(
                0.5 * sign * math.cos(angle) / math.sin(angle)
                + 0.25 * (-sign / (2.0 * math.sin(angle) ** 2))
            )
    return out


WEIGHTS = spectral_weights()


def spectral_kernel(x_ref, radius_ref, o_ref):
    start = CHUNK * lax.axis_index("inst")

    def body(t, carry):
        tile = start + t
        top = pl.multiple_of(8 * ((tile // TILES_W) % 2), 8)
        at = pl.multiple_of(LANES * (tile % TILES_W), LANES)
        scale = -0.5 / radius_ref[pl.ds(top, 8), pl.ds(at, LANES)]
        xs = [x_ref[m, t] for m in range(NT)]
        for n in range(NT):
            total = WEIGHTS[0] * xs[n]
            for k in range(1, NT):
                total = total + WEIGHTS[k] * xs[(n - k) % NT]
            o_ref[n, t] = scale * total
        return carry

    lax.fori_loop(0, CHUNK, body, 0, unroll=2)


def flux_kernel(
    mixing_ref, donor_ref, inter_ref, state_ref, radius_ref, up_ref, here_ref, down_ref, out_ref
):
    p = lax.axis_index("space")
    n = lax.axis_index("inst")
    row = lax.broadcasted_iota(jnp.int32, (8, LANES), 0)
    lane = lax.broadcasted_iota(jnp.int32, (8, LANES), 1)
    base = 2 * (p + 8 * n - 1)
    table = [jnp.zeros((8, LANES), jnp.float32) for _ in range(5)]
    for j in range(RI):
        w = inter_ref[0, j]
        first = (donor_ref[0, j, 0] - base + 2 * DONORS) % DONORS
        second = (donor_ref[0, j, 1] - base + 2 * DONORS) % DONORS
        for r in range(5):
            part = jnp.where(first == r, w, 0.0) + jnp.where(second == r, 1.0 - w, 0.0)
            table[r] = jnp.where(row == j, 2.0 * part, table[r])
    extra = jnp.where(row < RI, 2.0, 0.0)
    lo = jnp.where(p == 0, 0.0, 1.25)
    hi = jnp.where(p == SPACE - 1, 0.0, 0.25)
    mix = [[mixing_ref[v, u] for u in range(NV)] for v in range(NV)]

    def body(c, carry):
        at = pl.multiple_of(c * LANES, LANES)
        left = pl.multiple_of(jnp.maximum(c - 1, 0) * LANES, LANES)
        right = pl.multiple_of(jnp.minimum(c + 1, TILES_W - 1) * LANES, LANES)
        cols = pl.ds(at, LANES)
        wl = jnp.where(jnp.logical_and(c == 0, lane == 0), 0.0, 0.75)
        wr = jnp.where(jnp.logical_and(c == TILES_W - 1, lane == LANES - 1), 0.0, 0.25)
        scale = [0.5 / radius_ref[8 * h : 8 * h + 8, cols] for h in range(2)]
        cur = [[state_ref[0, v, 8 * h : 8 * h + 8, cols] for h in range(2)] for v in range(NV)]
        for v in range(NV):
            before = up_ref[v, 0:1, cols] * lo
            after = down_ref[v, 0:1, cols] * hi
            donors = [
                up_ref[v, 1:2, cols],
                up_ref[v, 2:3, cols],
                here_ref[v, 0:1, cols],
                here_ref[v, 1:2, cols],
                down_ref[v, 1:2, cols],
            ]
            c0, c1 = cur[v]
            xm = [
                jnp.where(row == 0, before, 1.25 * pltpu.roll(c0, 1, 0)),
                1.25 * pltpu.roll(jnp.where(row == 7, c0, c1), 1, 0),
            ]
            xp = [
                0.25 * pltpu.roll(jnp.where(row == 0, c1, c0), 7, 0),
                jnp.where(row == 7, after, 0.25 * pltpu.roll(c1, 7, 0)),
            ]
            for h in range(2):
                mine = cur[v][h]
                prev = state_ref[0, v, 8 * h : 8 * h + 8, pl.ds(left, LANES)]
                nxt = state_ref[0, v, 8 * h : 8 * h + 8, pl.ds(right, LANES)]
                wm = pltpu.roll(jnp.where(lane == LANES - 1, prev, mine), 1, 1)
                wp = pltpu.roll(jnp.where(lane == 0, nxt, mine), LANES - 1, 1)
                total = 2.5 * mine - xm[h] - xp[h] - wl * wm - wr * wp
                for u in range(NV):
                    total = total + mix[v][u] * cur[u][h]
                if h == 0:
                    total = total + extra * mine
                    for r in range(5):
                        total = total - table[r] * donors[r]
                out_ref[(v * 2 + h) * TILES_W + c] = mine - scale[h] * total
        return carry

    lax.fori_loop(0, TILES_W, body, 0)


def on_device(state, radius, mixing, donor, intersection):
    vmem = pl.BlockSpec(memory_space=pltpu.VMEM)
    smem = pl.BlockSpec(memory_space=pltpu.SMEM)
    limit = pltpu.CompilerParams(vmem_limit_bytes=8 * 1024 * 1024)
    field = state[0]
    tiles = field.reshape(NV, 2, 8, TILES_W, LANES).transpose(0, 1, 3, 2, 4).reshape(-1, 8, LANES)
    spread = lax.all_to_all(tiles, "inst", 0, 0, tiled=True)
    moves = [
        (n * SPACE + (p + 8 * n) % SPACE, n * SPACE + p) for n in range(NT) for p in range(SPACE)
    ]
    here = lax.ppermute(field[:, CX - 2 :], ("inst", "space"), moves)
    spread, here = lax.optimization_barrier((spread, here))

    up = lax.ppermute(
        jnp.concatenate([field[:, CX - 1 :], here], axis=1),
        "space",
        [(i, (i + 1) % SPACE) for i in range(SPACE)],
    )
    down = lax.ppermute(
        jnp.concatenate([field[:, :1], here[:, :1]], axis=1),
        "space",
        [((i + 1) % SPACE, i) for i in range(SPACE)],
    )
    mixed = pl.pallas_call(
        spectral_kernel,
        out_shape=jax.ShapeDtypeStruct((NT, CHUNK, 8, LANES), jnp.float32),
        in_specs=[vmem, vmem],
        out_specs=vmem,
        compiler_params=limit,
        cost_estimate=pl.CostEstimate(flops=3_000_000, bytes_accessed=1_700_000, transcendentals=0),
        name="spectral",
    )(spread.reshape(NT, CHUNK, 8, LANES), radius)
    spec = lax.all_to_all(mixed.reshape(-1, 8, LANES), "inst", 0, 0, tiled=True)
    kept = pl.pallas_call(
        flux_kernel,
        out_shape=jax.ShapeDtypeStruct(tiles.shape, jnp.float32),
        in_specs=[smem, smem, smem] + [vmem] * 5,
        out_specs=vmem,
        compiler_params=limit,
        cost_estimate=pl.CostEstimate(flops=6_000_000, bytes_accessed=2_000_000, transcendentals=0),
        name="flux",
    )(mixing, donor, intersection, state, radius, up, here, down)
    total = (kept + spec).reshape(NV, 2, TILES_W, 8, LANES).transpose(0, 1, 3, 2, 4)
    return total.reshape(state.shape)


def solution(mesh):
    in_specs = (
        P("inst", None, "space", None),
        P("space", None),
        P(),
        P("inst", "space", None),
        P("inst", "space"),
    )
    out_specs = P("inst", None, "space", None)
    return jax.shard_map(
        on_device, mesh=mesh, in_specs=in_specs, out_specs=out_specs, check_vma=False
    )
```

```python
import math

import jax
import jax.numpy as jnp
from jax import lax
from jax.experimental import pallas as pl
from jax.experimental.pallas import tpu as pltpu
from jax.sharding import PartitionSpec as P

NV = 6
CX = 16
CW = 2048
RI = 4
NT = 8
SPACE = 64
DONORS = 128
LANES = 128
TILES_W = CW // LANES
CHUNK = NV * CX * CW // (8 * LANES) // NT


def spectral_weights():
    out = []
    for k in range(NT):
        if k == 0:
            out.append(0.25 * (-(NT * NT + 2.0) / 12.0))
        else:
            sign = 1.0 - 2.0 * (k % 2)
            angle = math.pi * k / NT
            out.append(
                0.5 * sign * math.cos(angle) / math.sin(angle)
                + 0.25 * (-sign / (2.0 * math.sin(angle) ** 2))
            )
    return out


WEIGHTS = spectral_weights()


def spectral_kernel(x_ref, radius_ref, o_ref):
    start = CHUNK * lax.axis_index("inst")

    def body(t, carry):
        tile = start + t
        top = pl.multiple_of(8 * ((tile // TILES_W) % 2), 8)
        at = pl.multiple_of(LANES * (tile % TILES_W), LANES)
        scale = -0.5 / radius_ref[pl.ds(top, 8), pl.ds(at, LANES)]
        xs = [x_ref[m, t] for m in range(NT)]
        for n in range(NT):
            total = WEIGHTS[0] * xs[n]
            for k in range(1, NT):
                total = total + WEIGHTS[k] * xs[(n - k) % NT]
            o_ref[n, t] = scale * total
        return carry

    lax.fori_loop(0, CHUNK, body, 0, unroll=2)


def flux_kernel(mixing_ref, state_ref, radius_ref, out_ref):
    row = lax.broadcasted_iota(jnp.int32, (8, LANES), 0)
    lane = lax.broadcasted_iota(jnp.int32, (8, LANES), 1)
    extra = jnp.where(row < RI, 2.0, 0.0)
    mix = [[mixing_ref[v, u] for u in range(NV)] for v in range(NV)]

    def body(c, carry):
        at = pl.multiple_of(c * LANES, LANES)
        left = pl.multiple_of(jnp.maximum(c - 1, 0) * LANES, LANES)
        right = pl.multiple_of(jnp.minimum(c + 1, TILES_W - 1) * LANES, LANES)
        cols = pl.ds(at, LANES)
        wl = jnp.where(jnp.logical_and(c == 0, lane == 0), 0.0, 0.75)
        wr = jnp.where(jnp.logical_and(c == TILES_W - 1, lane == LANES - 1), 0.0, 0.25)
        scale = [0.5 / radius_ref[8 * h : 8 * h + 8, cols] for h in range(2)]
        cur = [[state_ref[0, v, 8 * h : 8 * h + 8, cols] for h in range(2)] for v in range(NV)]
        for v in range(NV):
            c0, c1 = cur[v]
            xm = [
                jnp.where(row == 0, 0.0, 1.25 * pltpu.roll(c0, 1, 0)),
                1.25 * pltpu.roll(jnp.where(row == 7, c0, c1), 1, 0),
            ]
            xp = [
                0.25 * pltpu.roll(jnp.where(row == 0, c1, c0), 7, 0),
                jnp.where(row == 7, 0.0, 0.25 * pltpu.roll(c1, 7, 0)),
            ]
            for h in range(2):
                mine = cur[v][h]
                prev = state_ref[0, v, 8 * h : 8 * h + 8, pl.ds(left, LANES)]
                nxt = state_ref[0, v, 8 * h : 8 * h + 8, pl.ds(right, LANES)]
                wm = pltpu.roll(jnp.where(lane == LANES - 1, prev, mine), 1, 1)
                wp = pltpu.roll(jnp.where(lane == 0, nxt, mine), LANES - 1, 1)
                total = 2.5 * mine - xm[h] - xp[h] - wl * wm - wr * wp
                for u in range(NV):
                    total = total + mix[v][u] * cur[u][h]
                if h == 0:
                    total = total + extra * mine
                out_ref[(v * 2 + h) * TILES_W + c] = mine - scale[h] * total
        return carry

    lax.fori_loop(0, TILES_W, body, 0)


def finish_kernel(
    donor_ref, inter_ref, radius_ref, kept_ref, spec_ref, up_ref, here_ref, down_ref, out_ref,
    held, sems,
):
    p = lax.axis_index("space")
    n = lax.axis_index("inst")
    row = lax.broadcasted_iota(jnp.int32, (8, LANES), 0)
    base = 2 * (p + 8 * n - 1)
    table = [jnp.zeros((8, LANES), jnp.float32) for _ in range(5)]
    for j in range(RI):
        w = inter_ref[0, j]
        first = (donor_ref[0, j, 0] - base + 2 * DONORS) % DONORS
        second = (donor_ref[0, j, 1] - base + 2 * DONORS) % DONORS
        for r in range(5):
            part = jnp.where(first == r, w, 0.0) + jnp.where(second == r, 1.0 - w, 0.0)
            table[r] = jnp.where(row == j, 2.0 * part, table[r])
    lo = jnp.where(row == 0, jnp.where(p == 0, 0.0, 1.25), 0.0)
    hi = jnp.where(row == 7, jnp.where(p == SPACE - 1, 0.0, 0.25), 0.0)
    span = 2 * TILES_W
    copies = []
    for v in range(NV):

        def body(c, carry):
            cols = pl.ds(pl.multiple_of(c * LANES, LANES), LANES)
            top = v * span + c
            bottom = top + TILES_W
            rows = [
                up_ref[v, 1:2, cols],
                up_ref[v, 2:3, cols],
                here_ref[v, 0:1, cols],
                here_ref[v, 1:2, cols],
                down_ref[v, 1:2, cols],
            ]
            fix = lo * up_ref[v, 0:1, cols]
            for r in range(5):
                fix = fix + table[r] * rows[r]
            scale = 0.5 / radius_ref[0:8, cols]
            held[top] = kept_ref[top] + spec_ref[top] + scale * fix
            scale = 0.5 / radius_ref[8:16, cols]
            held[bottom] = kept_ref[bottom] + spec_ref[bottom] + scale * (
                hi * down_ref[v, 0:1, cols]
            )
            return carry

        lax.fori_loop(0, TILES_W, body, 0, unroll=4)
        part = pl.ds(v * span, span)
        copies.append(pltpu.make_async_copy(held.at[part], out_ref.at[part], sems.at[v]))
        copies[-1].start()
    for copy in copies:
        copy.wait()


def on_device(state, radius, mixing, donor, intersection):
    vmem = pl.BlockSpec(memory_space=pltpu.VMEM)
    smem = pl.BlockSpec(memory_space=pltpu.SMEM)
    limit = pltpu.CompilerParams(vmem_limit_bytes=8 * 1024 * 1024)
    field = state[0]
    tiles = field.reshape(NV, 2, 8, TILES_W, LANES).transpose(0, 1, 3, 2, 4).reshape(-1, 8, LANES)
    moves = [
        (n * SPACE + (p + 8 * n) % SPACE, n * SPACE + p) for n in range(NT) for p in range(SPACE)
    ]
    here = lax.ppermute(field[:, CX - 2 :], ("inst", "space"), moves)
    spread = lax.all_to_all(tiles, "inst", 0, 0, tiled=True)

    kept = pl.pallas_call(
        flux_kernel,
        out_shape=jax.ShapeDtypeStruct(tiles.shape, jnp.float32),
        in_specs=[smem, vmem, vmem],
        out_specs=vmem,
        compiler_params=limit,
        cost_estimate=pl.CostEstimate(flops=6_000_000, bytes_accessed=2_000_000, transcendentals=0),
        name="flux",
    )(mixing, state, radius)
    spread, kept = lax.optimization_barrier((spread, kept))
    mixed = pl.pallas_call(
        spectral_kernel,
        out_shape=jax.ShapeDtypeStruct((NT, CHUNK, 8, LANES), jnp.float32),
        in_specs=[vmem, vmem],
        out_specs=vmem,
        compiler_params=limit,
        cost_estimate=pl.CostEstimate(flops=3_000_000, bytes_accessed=1_700_000, transcendentals=0),
        name="spectral",
    )(spread.reshape(NT, CHUNK, 8, LANES), radius)
    spec = lax.all_to_all(mixed.reshape(-1, 8, LANES), "inst", 0, 0, tiled=True)

    up = lax.ppermute(
        jnp.concatenate([field[:, CX - 1 :], here], axis=1),
        "space",
        [(i, (i + 1) % SPACE) for i in range(SPACE)],
    )
    down = lax.ppermute(
        jnp.concatenate([field[:, :1], here[:, :1]], axis=1),
        "space",
        [((i + 1) % SPACE, i) for i in range(SPACE)],
    )
    total = pl.pallas_call(
        finish_kernel,
        out_shape=jax.ShapeDtypeStruct(tiles.shape, jnp.float32),
        in_specs=[smem, smem] + [vmem] * 6,
        out_specs=pl.BlockSpec(memory_space=pl.ANY),
        scratch_shapes=[
            pltpu.VMEM(tiles.shape, jnp.float32),
            pltpu.SemaphoreType.DMA((NV,)),
        ],
        compiler_params=limit,
        cost_estimate=pl.CostEstimate(flops=3_000_000, bytes_accessed=2_500_000, transcendentals=0),
        name="finish",
    )(donor, intersection, radius, kept, spec, up, here, down)
    total = total.reshape(NV, 2, TILES_W, 8, LANES).transpose(0, 1, 3, 2, 4)
    return total.reshape(state.shape)


def solution(mesh):
    in_specs = (
        P("inst", None, "space", None),
        P("space", None),
        P(),
        P("inst", "space", None),
        P("inst", "space"),
    )
    out_specs = P("inst", None, "space", None)
    return jax.shard_map(
        on_device, mesh=mesh, in_specs=in_specs, out_specs=out_specs, check_vma=False
    )
```

```python
import math

import jax
import jax.numpy as jnp
from jax import lax
from jax.experimental import pallas as pl
from jax.experimental.pallas import tpu as pltpu
from jax.sharding import PartitionSpec as P

NV = 6
CX = 16
CW = 2048
RI = 4
NT = 8
SPACE = 64
DONORS = 128
LANES = 128
TILES_W = CW // LANES
CHUNK = NV * CX * CW // (8 * LANES) // NT


def spectral_weights():
    out = []
    for k in range(NT):
        if k == 0:
            out.append(0.25 * (-(NT * NT + 2.0) / 12.0))
        else:
            sign = 1.0 - 2.0 * (k % 2)
            angle = math.pi * k / NT
            out.append(
                0.5 * sign * math.cos(angle) / math.sin(angle)
                + 0.25 * (-sign / (2.0 * math.sin(angle) ** 2))
            )
    return out


WEIGHTS = spectral_weights()


def spectral_kernel(x_ref, radius_ref, o_ref):
    start = CHUNK * lax.axis_index("inst")

    def body(t, carry):
        tile = start + t
        top = pl.multiple_of(8 * ((tile // TILES_W) % 2), 8)
        at = pl.multiple_of(LANES * (tile % TILES_W), LANES)
        scale = -0.5 / radius_ref[pl.ds(top, 8), pl.ds(at, LANES)]
        xs = [x_ref[m, t] for m in range(NT)]
        for n in range(NT):
            total = WEIGHTS[0] * xs[n]
            for k in range(1, NT):
                total = total + WEIGHTS[k] * xs[(n - k) % NT]
            o_ref[n, t] = scale * total
        return carry

    lax.fori_loop(0, CHUNK, body, 0, unroll=2)


def flux_kernel(mixing_ref, state_ref, radius_ref, out_ref):
    row = lax.broadcasted_iota(jnp.int32, (8, LANES), 0)
    lane = lax.broadcasted_iota(jnp.int32, (8, LANES), 1)
    extra = jnp.where(row < RI, 2.0, 0.0)
    mix = [[mixing_ref[v, u] for u in range(NV)] for v in range(NV)]

    def body(c, carry):
        at = pl.multiple_of(c * LANES, LANES)
        left = pl.multiple_of(jnp.maximum(c - 1, 0) * LANES, LANES)
        right = pl.multiple_of(jnp.minimum(c + 1, TILES_W - 1) * LANES, LANES)
        cols = pl.ds(at, LANES)
        wl = jnp.where(jnp.logical_and(c == 0, lane == 0), 0.0, 0.75)
        wr = jnp.where(jnp.logical_and(c == TILES_W - 1, lane == LANES - 1), 0.0, 0.25)
        scale = [0.5 / radius_ref[8 * h : 8 * h + 8, cols] for h in range(2)]
        cur = [[state_ref[0, v, 8 * h : 8 * h + 8, cols] for h in range(2)] for v in range(NV)]
        for v in range(NV):
            c0, c1 = cur[v]
            xm = [
                jnp.where(row == 0, 0.0, 1.25 * pltpu.roll(c0, 1, 0)),
                1.25 * pltpu.roll(jnp.where(row == 7, c0, c1), 1, 0),
            ]
            xp = [
                0.25 * pltpu.roll(jnp.where(row == 0, c1, c0), 7, 0),
                jnp.where(row == 7, 0.0, 0.25 * pltpu.roll(c1, 7, 0)),
            ]
            for h in range(2):
                mine = cur[v][h]
                prev = state_ref[0, v, 8 * h : 8 * h + 8, pl.ds(left, LANES)]
                nxt = state_ref[0, v, 8 * h : 8 * h + 8, pl.ds(right, LANES)]
                wm = pltpu.roll(jnp.where(lane == LANES - 1, prev, mine), 1, 1)
                wp = pltpu.roll(jnp.where(lane == 0, nxt, mine), LANES - 1, 1)
                total = 2.5 * mine - xm[h] - xp[h] - wl * wm - wr * wp
                for u in range(NV):
                    total = total + mix[v][u] * cur[u][h]
                if h == 0:
                    total = total + extra * mine
                out_ref[(v * 2 + h) * TILES_W + c] = mine - scale[h] * total
        return carry

    lax.fori_loop(0, TILES_W, body, 0)


def finish_kernel(
    donor_ref, inter_ref, radius_ref, kept_ref, spec_ref, far_ref, chip_ref, pair_ref, out_ref,
    held, sems,
):
    p = lax.axis_index("space")
    n = lax.axis_index("inst")
    even = p % 2 == 0
    row = lax.broadcasted_iota(jnp.int32, (8, LANES), 0)
    base = 2 * (p + 8 * n - 1)
    zero = jnp.zeros((8, LANES), jnp.float32)
    table = [zero for _ in range(5)]
    for j in range(RI):
        w = inter_ref[0, j]
        first = (donor_ref[0, j, 0] - base + 2 * DONORS) % DONORS
        second = (donor_ref[0, j, 1] - base + 2 * DONORS) % DONORS
        for r in range(5):
            part = jnp.where(first == r, w, 0.0) + jnp.where(second == r, 1.0 - w, 0.0)
            table[r] = jnp.where(row == j, 2.0 * part, table[r])
    far0 = jnp.where(even, table[0], table[4])
    far1 = jnp.where(even, table[1], zero)
    pair0 = jnp.where(even, table[4], table[0])
    pair1 = jnp.where(even, zero, table[1])
    lo = jnp.where(row == 0, jnp.where(p == 0, 0.0, 1.25), 0.0)
    hi = jnp.where(row == 7, jnp.where(p == SPACE - 1, 0.0, 0.25), 0.0)
    lo_chip, lo_pair = jnp.where(even, lo, zero), jnp.where(even, zero, lo)
    hi_chip, hi_pair = jnp.where(even, zero, hi), jnp.where(even, hi, zero)
    span = 2 * TILES_W
    copies = []
    for v in range(NV):

        def body(c, carry):
            cols = pl.ds(pl.multiple_of(c * LANES, LANES), LANES)
            top = v * span + c
            bottom = top + TILES_W
            chip_edge = chip_ref[v, 0:1, cols]
            pair_edge = pair_ref[v, 0:1, cols]
            fix = lo_chip * chip_edge + lo_pair * pair_edge
            fix = fix + far0 * far_ref[v, 0:1, cols] + far1 * far_ref[v, 1:2, cols]
            fix = fix + table[2] * chip_ref[v, 1:2, cols] + table[3] * chip_ref[v, 2:3, cols]
            fix = fix + pair0 * pair_ref[v, 1:2, cols] + pair1 * pair_ref[v, 2:3, cols]
            scale = 0.5 / radius_ref[0:8, cols]
            held[top] = kept_ref[top] + spec_ref[top] + scale * fix
            scale = 0.5 / radius_ref[8:16, cols]
            held[bottom] = kept_ref[bottom] + spec_ref[bottom] + scale * (
                hi_chip * chip_edge + hi_pair * pair_edge
            )
            return carry

        lax.fori_loop(0, TILES_W, body, 0, unroll=4)
        part = pl.ds(v * span, span)
        copies.append(pltpu.make_async_copy(held.at[part], out_ref.at[part], sems.at[v]))
        copies[-1].start()
    for copy in copies:
        copy.wait()


def on_device(state, radius, mixing, donor, intersection):
    vmem = pl.BlockSpec(memory_space=pltpu.VMEM)
    smem = pl.BlockSpec(memory_space=pltpu.SMEM)
    limit = pltpu.CompilerParams(vmem_limit_bytes=8 * 1024 * 1024)
    field = state[0]
    tiles = field.reshape(NV, 2, 8, TILES_W, LANES).transpose(0, 1, 3, 2, 4).reshape(-1, 8, LANES)
    even = lax.axis_index("space") % 2 == 0
    moves = [
        (n * SPACE + (p + 8 * n + 2 * (p % 2) - 1) % SPACE, n * SPACE + p)
        for n in range(NT)
        for p in range(SPACE)
    ]
    far = lax.ppermute(field[:, CX - 2 :], ("inst", "space"), moves)
    spread = lax.all_to_all(tiles, "inst", 0, 0, tiled=True)

    mixed = pl.pallas_call(
        spectral_kernel,
        out_shape=jax.ShapeDtypeStruct((NT, CHUNK, 8, LANES), jnp.float32),
        in_specs=[vmem, vmem],
        out_specs=vmem,
        compiler_params=limit,
        cost_estimate=pl.CostEstimate(flops=3_000_000, bytes_accessed=1_700_000, transcendentals=0),
        name="spectral",
    )(spread.reshape(NT, CHUNK, 8, LANES), radius)
    spec = lax.all_to_all(mixed.reshape(-1, 8, LANES), "inst", 0, 0, tiled=True)

    first, last = field[:, :1], field[:, CX - 1 :]
    chip = lax.ppermute(
        jnp.concatenate([jnp.where(even, first, last), far], axis=1),
        "space",
        [(p, (p + 2 * (p % 2) - 1) % SPACE) for p in range(SPACE)],
    )
    pair = lax.ppermute(
        jnp.concatenate([jnp.where(even, last, first), chip[:, 1:]], axis=1),
        "space",
        [(p, p ^ 1) for p in range(SPACE)],
    )
    kept = pl.pallas_call(
        flux_kernel,
        out_shape=jax.ShapeDtypeStruct(tiles.shape, jnp.float32),
        in_specs=[smem, vmem, vmem],
        out_specs=vmem,
        compiler_params=limit,
        cost_estimate=pl.CostEstimate(flops=6_000_000, bytes_accessed=2_000_000, transcendentals=0),
        name="flux",
    )(mixing, state, radius)
    total = pl.pallas_call(
        finish_kernel,
        out_shape=jax.ShapeDtypeStruct(tiles.shape, jnp.float32),
        in_specs=[smem, smem] + [vmem] * 6,
        out_specs=pl.BlockSpec(memory_space=pl.ANY),
        scratch_shapes=[
            pltpu.VMEM(tiles.shape, jnp.float32),
            pltpu.SemaphoreType.DMA((NV,)),
        ],
        compiler_params=limit,
        cost_estimate=pl.CostEstimate(flops=3_000_000, bytes_accessed=2_500_000, transcendentals=0),
        name="finish",
    )(donor, intersection, radius, kept, spec, far, chip, pair)
    total = total.reshape(NV, 2, TILES_W, 8, LANES).transpose(0, 1, 3, 2, 4)
    return total.reshape(state.shape)


def solution(mesh):
    in_specs = (
        P("inst", None, "space", None),
        P("space", None),
        P(),
        P("inst", "space", None),
        P("inst", "space"),
    )
    out_specs = P("inst", None, "space", None)
    return jax.shard_map(
        on_device, mesh=mesh, in_specs=in_specs, out_specs=out_specs, check_vma=False
    )
```

```python
import math

import jax
import jax.numpy as jnp
from jax import lax
from jax.experimental import pallas as pl
from jax.experimental.pallas import tpu as pltpu
from jax.sharding import PartitionSpec as P

NV = 6
CX = 16
CW = 2048
RI = 4
NT = 8
SPACE = 64
DONORS = 128
LANES = 128
TILES_W = CW // LANES
CHUNK = NV * CX * CW // (8 * LANES) // NT


def spectral_weights():
    out = []
    for k in range(NT):
        if k == 0:
            out.append(0.25 * (-(NT * NT + 2.0) / 12.0))
        else:
            sign = 1.0 - 2.0 * (k % 2)
            angle = math.pi * k / NT
            out.append(
                0.5 * sign * math.cos(angle) / math.sin(angle)
                + 0.25 * (-sign / (2.0 * math.sin(angle) ** 2))
            )
    return out


WEIGHTS = spectral_weights()


def spectral_kernel(x_ref, radius_ref, o_ref):
    start = CHUNK * lax.axis_index("inst")

    def body(t, carry):
        tile = start + t
        top = pl.multiple_of(8 * ((tile // TILES_W) % 2), 8)
        at = pl.multiple_of(LANES * (tile % TILES_W), LANES)
        scale = -0.5 / radius_ref[pl.ds(top, 8), pl.ds(at, LANES)]
        xs = [x_ref[m, t] for m in range(NT)]
        for n in range(NT):
            total = WEIGHTS[0] * xs[n]
            for k in range(1, NT):
                total = total + WEIGHTS[k] * xs[(n - k) % NT]
            o_ref[n, t] = scale * total
        return carry

    lax.fori_loop(0, CHUNK, body, 0, unroll=2)


def flux_kernel(mixing_ref, state_ref, radius_ref, out_ref):
    row = lax.broadcasted_iota(jnp.int32, (8, LANES), 0)
    lane = lax.broadcasted_iota(jnp.int32, (8, LANES), 1)
    extra = jnp.where(row < RI, 2.0, 0.0)
    mix = [[mixing_ref[v, u] for u in range(NV)] for v in range(NV)]

    def body(c, carry):
        at = pl.multiple_of(c * LANES, LANES)
        left = pl.multiple_of(jnp.maximum(c - 1, 0) * LANES, LANES)
        right = pl.multiple_of(jnp.minimum(c + 1, TILES_W - 1) * LANES, LANES)
        cols = pl.ds(at, LANES)
        wl = jnp.where(jnp.logical_and(c == 0, lane == 0), 0.0, 0.75)
        wr = jnp.where(jnp.logical_and(c == TILES_W - 1, lane == LANES - 1), 0.0, 0.25)
        scale = [0.5 / radius_ref[8 * h : 8 * h + 8, cols] for h in range(2)]
        cur = [[state_ref[0, v, 8 * h : 8 * h + 8, cols] for h in range(2)] for v in range(NV)]
        for v in range(NV):
            c0, c1 = cur[v]
            xm = [
                jnp.where(row == 0, 0.0, 1.25 * pltpu.roll(c0, 1, 0)),
                1.25 * pltpu.roll(jnp.where(row == 7, c0, c1), 1, 0),
            ]
            xp = [
                0.25 * pltpu.roll(jnp.where(row == 0, c1, c0), 7, 0),
                jnp.where(row == 7, 0.0, 0.25 * pltpu.roll(c1, 7, 0)),
            ]
            for h in range(2):
                mine = cur[v][h]
                prev = state_ref[0, v, 8 * h : 8 * h + 8, pl.ds(left, LANES)]
                nxt = state_ref[0, v, 8 * h : 8 * h + 8, pl.ds(right, LANES)]
                wm = pltpu.roll(jnp.where(lane == LANES - 1, prev, mine), 1, 1)
                wp = pltpu.roll(jnp.where(lane == 0, nxt, mine), LANES - 1, 1)
                total = 2.5 * mine - xm[h] - xp[h] - wl * wm - wr * wp
                for u in range(NV):
                    total = total + mix[v][u] * cur[u][h]
                if h == 0:
                    total = total + extra * mine
                out_ref[(v * 2 + h) * TILES_W + c] = mine - scale[h] * total
        return carry

    lax.fori_loop(0, TILES_W, body, 0)


def finish_kernel(
    donor_ref, inter_ref, radius_ref, kept_ref, spec_ref, far_ref, chip_ref, pair_ref, out_ref,
    held, sems,
):
    p = lax.axis_index("space")
    n = lax.axis_index("inst")
    even = p % 2 == 0
    row = lax.broadcasted_iota(jnp.int32, (8, LANES), 0)
    base = 2 * (p + 8 * n - 1)
    zero = jnp.zeros((8, LANES), jnp.float32)
    table = [zero for _ in range(5)]
    for j in range(RI):
        w = inter_ref[0, j]
        first = (donor_ref[0, j, 0] - base + 2 * DONORS) % DONORS
        second = (donor_ref[0, j, 1] - base + 2 * DONORS) % DONORS
        for r in range(5):
            part = jnp.where(first == r, w, 0.0) + jnp.where(second == r, 1.0 - w, 0.0)
            table[r] = jnp.where(row == j, 2.0 * part, table[r])
    far0 = jnp.where(even, table[0], table[4])
    far1 = jnp.where(even, table[1], zero)
    pair0 = jnp.where(even, table[4], table[0])
    pair1 = jnp.where(even, zero, table[1])
    lo = jnp.where(row == 0, jnp.where(p == 0, 0.0, 1.25), 0.0)
    hi = jnp.where(row == 7, jnp.where(p == SPACE - 1, 0.0, 0.25), 0.0)
    lo_chip, lo_pair = jnp.where(even, lo, zero), jnp.where(even, zero, lo)
    hi_chip, hi_pair = jnp.where(even, zero, hi), jnp.where(even, hi, zero)
    span = 2 * TILES_W
    copies = []
    for v in range(NV):

        def body(c, carry):
            cols = pl.ds(pl.multiple_of(c * LANES, LANES), LANES)
            top = v * span + c
            bottom = top + TILES_W
            chip_edge = chip_ref[v, 0:1, cols]
            pair_edge = pair_ref[v, 0:1, cols]
            fix = lo_chip * chip_edge + lo_pair * pair_edge
            fix = fix + far0 * far_ref[v, 0:1, cols] + far1 * far_ref[v, 1:2, cols]
            fix = fix + table[2] * chip_ref[v, 1:2, cols] + table[3] * chip_ref[v, 2:3, cols]
            fix = fix + pair0 * pair_ref[v, 1:2, cols] + pair1 * pair_ref[v, 2:3, cols]
            scale = 0.5 / radius_ref[0:8, cols]
            held[top] = kept_ref[top] + spec_ref[top] + scale * fix
            scale = 0.5 / radius_ref[8:16, cols]
            held[bottom] = kept_ref[bottom] + spec_ref[bottom] + scale * (
                hi_chip * chip_edge + hi_pair * pair_edge
            )
            return carry

        lax.fori_loop(0, TILES_W, body, 0, unroll=4)
        part = pl.ds(v * span, span)
        copies.append(pltpu.make_async_copy(held.at[part], out_ref.at[part], sems.at[v]))
        copies[-1].start()
    for copy in copies:
        copy.wait()


def on_device(state, radius, mixing, donor, intersection):
    vmem = pl.BlockSpec(memory_space=pltpu.VMEM)
    smem = pl.BlockSpec(memory_space=pltpu.SMEM)
    limit = pltpu.CompilerParams(vmem_limit_bytes=8 * 1024 * 1024)
    field = state[0]
    tiles = field.reshape(NV, 2, 8, TILES_W, LANES).transpose(0, 1, 3, 2, 4).reshape(-1, 8, LANES)
    even = lax.axis_index("space") % 2 == 0
    moves = [
        (n * SPACE + (p + 8 * n + 2 * (p % 2) - 1) % SPACE, n * SPACE + p)
        for n in range(NT)
        for p in range(SPACE)
    ]
    far = lax.ppermute(field[:, CX - 2 :], ("inst", "space"), moves)
    spread = lax.all_to_all(tiles, "inst", 0, 0, tiled=True)

    mixed = pl.pallas_call(
        spectral_kernel,
        out_shape=jax.ShapeDtypeStruct((NT, CHUNK, 8, LANES), jnp.float32),
        in_specs=[vmem, vmem],
        out_specs=vmem,
        compiler_params=limit,
        cost_estimate=pl.CostEstimate(flops=3_000_000, bytes_accessed=1_700_000, transcendentals=0),
        name="spectral",
    )(spread.reshape(NT, CHUNK, 8, LANES), radius)
    spec = lax.all_to_all(mixed.reshape(-1, 8, LANES), "inst", 0, 0, tiled=True)

    first, last = field[:, :1], field[:, CX - 1 :]
    chip = lax.ppermute(
        jnp.concatenate([jnp.where(even, first, last), far], axis=1),
        "space",
        [(p, (p + 2 * (p % 2) - 1) % SPACE) for p in range(SPACE)],
    )
    kept = pl.pallas_call(
        flux_kernel,
        out_shape=jax.ShapeDtypeStruct(tiles.shape, jnp.float32),
        in_specs=[smem, vmem, vmem],
        out_specs=vmem,
        compiler_params=limit,
        cost_estimate=pl.CostEstimate(flops=6_000_000, bytes_accessed=2_000_000, transcendentals=0),
        name="flux",
    )(mixing, state, radius)
    chip, kept = lax.optimization_barrier((chip, kept))
    pair = lax.ppermute(
        jnp.concatenate([jnp.where(even, last, first), chip[:, 1:]], axis=1),
        "space",
        [(p, p ^ 1) for p in range(SPACE)],
    )
    total = pl.pallas_call(
        finish_kernel,
        out_shape=jax.ShapeDtypeStruct(tiles.shape, jnp.float32),
        in_specs=[smem, smem] + [vmem] * 6,
        out_specs=pl.BlockSpec(memory_space=pl.ANY),
        scratch_shapes=[
            pltpu.VMEM(tiles.shape, jnp.float32),
            pltpu.SemaphoreType.DMA((NV,)),
        ],
        compiler_params=limit,
        cost_estimate=pl.CostEstimate(flops=3_000_000, bytes_accessed=2_500_000, transcendentals=0),
        name="finish",
    )(donor, intersection, radius, kept, spec, far, chip, pair)
    total = total.reshape(NV, 2, TILES_W, 8, LANES).transpose(0, 1, 3, 2, 4)
    return total.reshape(state.shape)


def solution(mesh):
    in_specs = (
        P("inst", None, "space", None),
        P("space", None),
        P(),
        P("inst", "space", None),
        P("inst", "space"),
    )
    out_specs = P("inst", None, "space", None)
    return jax.shard_map(
        on_device, mesh=mesh, in_specs=in_specs, out_specs=out_specs, check_vma=False
    )
```

```python
import math

import jax
import jax.numpy as jnp
from jax import lax
from jax.experimental import pallas as pl
from jax.experimental.pallas import tpu as pltpu
from jax.sharding import PartitionSpec as P

NV = 6
CX = 16
CW = 2048
RI = 4
NT = 8
SPACE = 64
DONORS = 128
LANES = 128
TILES_W = CW // LANES
HALF = SPACE // 2
PARTS = 4
CHUNK = NV * CX * CW // (8 * LANES) // NT


def spectral_weights():
    out = []
    for k in range(NT):
        if k == 0:
            out.append(0.25 * (-(NT * NT + 2.0) / 12.0))
        else:
            sign = 1.0 - 2.0 * (k % 2)
            angle = math.pi * k / NT
            out.append(
                0.5 * sign * math.cos(angle) / math.sin(angle)
                + 0.25 * (-sign / (2.0 * math.sin(angle) ** 2))
            )
    return out


WEIGHTS = spectral_weights()


def spectral_kernel(x_ref, radius_ref, o_ref, held, sems):
    start = CHUNK * lax.axis_index("inst")

    def body(t, carry):
        tile = start + t
        top = pl.multiple_of(8 * ((tile // TILES_W) % 2), 8)
        at = pl.multiple_of(LANES * (tile % TILES_W), LANES)
        scale = -0.5 / radius_ref[pl.ds(top, 8), pl.ds(at, LANES)]
        xs = [x_ref[m, t] for m in range(NT)]
        for n in range(NT):
            total = WEIGHTS[0] * xs[n]
            for k in range(1, NT):
                total = total + WEIGHTS[k] * xs[(n - k) % NT]
            held[n, t] = scale * total
        return carry

    copies = []
    for part in range(PARTS):
        here = CHUNK // PARTS * part
        lax.fori_loop(here, here + CHUNK // PARTS, body, 0, unroll=2)
        rows = pl.ds(here, CHUNK // PARTS)
        copies.append(pltpu.make_async_copy(held.at[:, rows], o_ref.at[:, rows], sems.at[part]))
        copies[-1].start()
    for copy in copies:
        copy.wait()


def flux_kernel(mixing_ref, state_ref, radius_ref, out_ref):
    row = lax.broadcasted_iota(jnp.int32, (8, LANES), 0)
    lane = lax.broadcasted_iota(jnp.int32, (8, LANES), 1)
    extra = jnp.where(row < RI, 2.0, 0.0)
    mix = [[mixing_ref[v, u] for u in range(NV)] for v in range(NV)]

    def body(c, carry):
        at = pl.multiple_of(c * LANES, LANES)
        left = pl.multiple_of(jnp.maximum(c - 1, 0) * LANES, LANES)
        right = pl.multiple_of(jnp.minimum(c + 1, TILES_W - 1) * LANES, LANES)
        cols = pl.ds(at, LANES)
        wl = jnp.where(jnp.logical_and(c == 0, lane == 0), 0.0, 0.75)
        wr = jnp.where(jnp.logical_and(c == TILES_W - 1, lane == LANES - 1), 0.0, 0.25)
        scale = [0.5 / radius_ref[8 * h : 8 * h + 8, cols] for h in range(2)]
        cur = [[state_ref[0, v, 8 * h : 8 * h + 8, cols] for h in range(2)] for v in range(NV)]
        for v in range(NV):
            c0, c1 = cur[v]
            xm = [
                jnp.where(row == 0, 0.0, 1.25 * pltpu.roll(c0, 1, 0)),
                1.25 * pltpu.roll(jnp.where(row == 7, c0, c1), 1, 0),
            ]
            xp = [
                0.25 * pltpu.roll(jnp.where(row == 0, c1, c0), 7, 0),
                jnp.where(row == 7, 0.0, 0.25 * pltpu.roll(c1, 7, 0)),
            ]
            for h in range(2):
                mine = cur[v][h]
                prev = state_ref[0, v, 8 * h : 8 * h + 8, pl.ds(left, LANES)]
                nxt = state_ref[0, v, 8 * h : 8 * h + 8, pl.ds(right, LANES)]
                wm = pltpu.roll(jnp.where(lane == LANES - 1, prev, mine), 1, 1)
                wp = pltpu.roll(jnp.where(lane == 0, nxt, mine), LANES - 1, 1)
                total = 2.5 * mine - xm[h] - xp[h] - wl * wm - wr * wp
                for u in range(NV):
                    total = total + mix[v][u] * cur[u][h]
                if h == 0:
                    total = total + extra * mine
                out_ref[(v * 2 + h) * TILES_W + c] = mine - scale[h] * total
        return carry

    lax.fori_loop(0, TILES_W, body, 0)


def pack_kernel(state_ref, chip_ref, fall_ref, chip_out_ref, pair_out_ref):
    even = lax.axis_index("space") % 2 == 0
    for v in range(NV):
        direct = fall_ref[v]
        own = chip_ref[v, 1:3] + jnp.where(even, direct, 0.0)
        chip_out_ref[v, 0:1] = chip_ref[v, 0:1]
        chip_out_ref[v, 1:3] = own
        pair_out_ref[v, 0:1] = jnp.where(even, state_ref[0, v, CX - 1 : CX], state_ref[0, v, 0:1])
        pair_out_ref[v, 1:3] = own
        pair_out_ref[v, 3:4] = jnp.where(even, 0.0, direct[1:2])


def fix_kernel(
    donor_ref, inter_ref, radius_ref, kept_ref, far_ref, chip_ref, pair_ref, out_ref
):
    p = lax.axis_index("space")
    n = lax.axis_index("inst")
    even = p % 2 == 0
    row = lax.broadcasted_iota(jnp.int32, (8, LANES), 0)
    base = 2 * (p + 8 * n - 1)
    zero = jnp.zeros((8, LANES), jnp.float32)
    table = [zero for _ in range(5)]
    for j in range(RI):
        w = inter_ref[0, j]
        first = (donor_ref[0, j, 0] - base + 2 * DONORS) % DONORS
        second = (donor_ref[0, j, 1] - base + 2 * DONORS) % DONORS
        for r in range(5):
            part = jnp.where(first == r, w, 0.0) + jnp.where(second == r, 1.0 - w, 0.0)
            table[r] = jnp.where(row == j, 2.0 * part, table[r])
    far0 = jnp.where(even, table[0], table[4])
    far1 = jnp.where(even, table[1], zero)
    pair0 = jnp.where(even, table[4], table[0])
    pair1 = jnp.where(even, zero, table[1])
    lo = jnp.where(row == 0, jnp.where(p == 0, 0.0, 1.25), 0.0)
    hi = jnp.where(row == 7, jnp.where(p == SPACE - 1, 0.0, 0.25), 0.0)
    lo_chip, lo_pair = jnp.where(even, lo, zero), jnp.where(even, zero, lo)
    hi_chip, hi_pair = jnp.where(even, zero, hi), jnp.where(even, hi, zero)
    span = 2 * TILES_W
    for v in range(NV):

        def body(c, carry):
            cols = pl.ds(pl.multiple_of(c * LANES, LANES), LANES)
            top = v * span + c
            bottom = top + TILES_W
            chip_edge = chip_ref[v, 0:1, cols] + pair_ref[v, 3:4, cols]
            pair_edge = pair_ref[v, 0:1, cols]
            fix = lo_chip * chip_edge + lo_pair * pair_edge
            fix = fix + far0 * far_ref[v, 0:1, cols] + far1 * far_ref[v, 1:2, cols]
            fix = fix + table[2] * chip_ref[v, 1:2, cols] + table[3] * chip_ref[v, 2:3, cols]
            fix = fix + pair0 * pair_ref[v, 1:2, cols] + pair1 * pair_ref[v, 2:3, cols]
            scale = 0.5 / radius_ref[0:8, cols]
            out_ref[top] = kept_ref[top] + scale * fix
            scale = 0.5 / radius_ref[8:16, cols]
            out_ref[bottom] = kept_ref[bottom] + scale * (
                hi_chip * chip_edge + hi_pair * pair_edge
            )
            return carry

        lax.fori_loop(0, TILES_W, body, 0, unroll=4)


def add_kernel(kept_ref, spec_ref, out_ref, held, sems):
    span = 2 * TILES_W
    copies = []
    for v in range(NV):

        def body(t, carry):
            held[v * span + t] = kept_ref[v * span + t] + spec_ref[v * span + t]
            return carry

        lax.fori_loop(0, span, body, 0, unroll=8)
        part = pl.ds(v * span, span)
        copies.append(pltpu.make_async_copy(held.at[part], out_ref.at[part], sems.at[v]))
        copies[-1].start()
    for copy in copies:
        copy.wait()


def on_device(state, radius, mixing, donor, intersection):
    vmem = pl.BlockSpec(memory_space=pltpu.VMEM)
    smem = pl.BlockSpec(memory_space=pltpu.SMEM)
    limit = pltpu.CompilerParams(vmem_limit_bytes=8 * 1024 * 1024)
    field = state[0]
    tiles = field.reshape(NV, 2, 8, TILES_W, LANES).transpose(0, 1, 3, 2, 4).reshape(-1, 8, LANES)
    even = lax.axis_index("space") % 2 == 0
    moves = [
        (n * SPACE + (p + 8 * n + 2 * (p % 2) - 1) % SPACE, n * SPACE + p)
        for n in range(NT)
        for p in range(SPACE)
    ]
    donors = field[:, CX - 2 :]
    direct = [(n * SPACE + (p + 8 * n) % SPACE, n * SPACE + p) for n in range(NT) for p in (0, HALF)]
    direct += [(n * SPACE + HALF - 1, n * SPACE + HALF + 1) for n in range(NT)]
    fall = lax.ppermute(donors, ("inst", "space"), direct)
    far = lax.ppermute(donors, ("inst", "space"), moves)
    spread = lax.all_to_all(tiles, "inst", 0, 0, tiled=True)

    mixed = pl.pallas_call(
        spectral_kernel,
        out_shape=jax.ShapeDtypeStruct((NT, CHUNK, 8, LANES), jnp.float32),
        in_specs=[vmem, vmem],
        out_specs=pl.BlockSpec(memory_space=pl.ANY),
        scratch_shapes=[
            pltpu.VMEM((NT, CHUNK, 8, LANES), jnp.float32),
            pltpu.SemaphoreType.DMA((PARTS,)),
        ],
        compiler_params=limit,
        cost_estimate=pl.CostEstimate(flops=3_000_000, bytes_accessed=1_700_000, transcendentals=0),
        name="spectral",
    )(spread.reshape(NT, CHUNK, 8, LANES), radius)
    spec = lax.all_to_all(mixed.reshape(-1, 8, LANES), "inst", 0, 0, tiled=True)

    far, fall = lax.optimization_barrier((far, fall))
    first, last = field[:, :1], field[:, CX - 1 :]
    chip = lax.ppermute(
        jnp.concatenate([jnp.where(even, first, last), far], axis=1),
        "space",
        [
            (p, (p + 2 * (p % 2) - 1) % SPACE)
            for p in range(SPACE)
            if p not in (HALF - 1, SPACE - 1)
        ],
    )
    kept = pl.pallas_call(
        flux_kernel,
        out_shape=jax.ShapeDtypeStruct(tiles.shape, jnp.float32),
        in_specs=[smem, vmem, vmem],
        out_specs=vmem,
        compiler_params=limit,
        cost_estimate=pl.CostEstimate(flops=6_000_000, bytes_accessed=2_000_000, transcendentals=0),
        name="flux",
    )(mixing, state, radius)
    chip, kept = lax.optimization_barrier((chip, kept))
    chip, pair_send = pl.pallas_call(
        pack_kernel,
        out_shape=[
            jax.ShapeDtypeStruct((NV, 3, CW), jnp.float32),
            jax.ShapeDtypeStruct((NV, 4, CW), jnp.float32),
        ],
        in_specs=[vmem] * 3,
        out_specs=[vmem] * 2,
        compiler_params=limit,
        cost_estimate=pl.CostEstimate(flops=100_000, bytes_accessed=800_000, transcendentals=0),
        name="pack",
    )(state, chip, fall)
    pair = lax.ppermute(pair_send, "space", [(p, p ^ 1) for p in range(SPACE)])
    fixed = pl.pallas_call(
        fix_kernel,
        out_shape=jax.ShapeDtypeStruct(tiles.shape, jnp.float32),
        in_specs=[smem, smem] + [vmem] * 5,
        out_specs=vmem,
        compiler_params=limit,
        cost_estimate=pl.CostEstimate(flops=3_000_000, bytes_accessed=2_000_000, transcendentals=0),
        name="fix",
    )(donor, intersection, radius, kept, far, chip, pair)
    fixed, spec = lax.optimization_barrier((fixed, spec))
    total = pl.pallas_call(
        add_kernel,
        out_shape=jax.ShapeDtypeStruct(tiles.shape, jnp.float32),
        in_specs=[vmem] * 2,
        out_specs=pl.BlockSpec(memory_space=pl.ANY),
        scratch_shapes=[
            pltpu.VMEM(tiles.shape, jnp.float32),
            pltpu.SemaphoreType.DMA((NV,)),
        ],
        compiler_params=limit,
        cost_estimate=pl.CostEstimate(flops=200_000, bytes_accessed=2_400_000, transcendentals=0),
        name="add",
    )(fixed, spec)
    total = total.reshape(NV, 2, TILES_W, 8, LANES).transpose(0, 1, 3, 2, 4)
    return total.reshape(state.shape)


def solution(mesh):
    in_specs = (
        P("inst", None, "space", None),
        P("space", None),
        P(),
        P("inst", "space", None),
        P("inst", "space"),
    )
    out_specs = P("inst", None, "space", None)
    return jax.shard_map(
        on_device, mesh=mesh, in_specs=in_specs, out_specs=out_specs, check_vma=False
    )
```

```python
import math

import jax
import jax.numpy as jnp
from jax import lax
from jax.experimental import pallas as pl
from jax.experimental.pallas import tpu as pltpu
from jax.sharding import PartitionSpec as P

NV = 6
CX = 16
CW = 2048
RI = 4
NT = 8
SPACE = 64
DONORS = 128
LANES = 128
TILES_W = CW // LANES
HALF = SPACE // 2
PARTS = 8
CHUNK = NV * CX * CW // (8 * LANES) // NT


def spectral_weights():
    out = []
    for k in range(NT):
        if k == 0:
            out.append(0.25 * (-(NT * NT + 2.0) / 12.0))
        else:
            sign = 1.0 - 2.0 * (k % 2)
            angle = math.pi * k / NT
            out.append(
                0.5 * sign * math.cos(angle) / math.sin(angle)
                + 0.25 * (-sign / (2.0 * math.sin(angle) ** 2))
            )
    return out


WEIGHTS = spectral_weights()


def spectral_kernel(x_ref, radius_ref, o_ref, held, sems):
    start = CHUNK * lax.axis_index("inst")

    def body(t, carry):
        tile = start + t
        top = pl.multiple_of(8 * ((tile // TILES_W) % 2), 8)
        at = pl.multiple_of(LANES * (tile % TILES_W), LANES)
        scale = -0.5 / radius_ref[pl.ds(top, 8), pl.ds(at, LANES)]
        xs = [x_ref[m, t] for m in range(NT)]
        for n in range(NT):
            total = WEIGHTS[0] * xs[n]
            for k in range(1, NT):
                total = total + WEIGHTS[k] * xs[(n - k) % NT]
            held[n, t] = scale * total
        return carry

    copies = []
    for part in range(PARTS):
        here = CHUNK // PARTS * part
        lax.fori_loop(here, here + CHUNK // PARTS, body, 0, unroll=3)
        rows = pl.ds(here, CHUNK // PARTS)
        copies.append(pltpu.make_async_copy(held.at[:, rows], o_ref.at[:, rows], sems.at[part]))
        copies[-1].start()
    for copy in copies:
        copy.wait()


def flux_kernel(mixing_ref, state_ref, radius_ref, out_ref):
    row = lax.broadcasted_iota(jnp.int32, (8, LANES), 0)
    lane = lax.broadcasted_iota(jnp.int32, (8, LANES), 1)
    extra = jnp.where(row < RI, 2.0, 0.0)
    mix = [[mixing_ref[v, u] for u in range(NV)] for v in range(NV)]

    def body(c, carry):
        at = pl.multiple_of(c * LANES, LANES)
        left = pl.multiple_of(jnp.maximum(c - 1, 0) * LANES, LANES)
        right = pl.multiple_of(jnp.minimum(c + 1, TILES_W - 1) * LANES, LANES)
        cols = pl.ds(at, LANES)
        wl = jnp.where(jnp.logical_and(c == 0, lane == 0), 0.0, 0.75)
        wr = jnp.where(jnp.logical_and(c == TILES_W - 1, lane == LANES - 1), 0.0, 0.25)
        scale = [0.5 / radius_ref[8 * h : 8 * h + 8, cols] for h in range(2)]
        cur = [[state_ref[0, v, 8 * h : 8 * h + 8, cols] for h in range(2)] for v in range(NV)]
        for v in range(NV):
            c0, c1 = cur[v]
            xm = [
                jnp.where(row == 0, 0.0, 1.25 * pltpu.roll(c0, 1, 0)),
                1.25 * pltpu.roll(jnp.where(row == 7, c0, c1), 1, 0),
            ]
            xp = [
                0.25 * pltpu.roll(jnp.where(row == 0, c1, c0), 7, 0),
                jnp.where(row == 7, 0.0, 0.25 * pltpu.roll(c1, 7, 0)),
            ]
            for h in range(2):
                mine = cur[v][h]
                prev = state_ref[0, v, 8 * h : 8 * h + 8, pl.ds(left, LANES)]
                nxt = state_ref[0, v, 8 * h : 8 * h + 8, pl.ds(right, LANES)]
                wm = pltpu.roll(jnp.where(lane == LANES - 1, prev, mine), 1, 1)
                wp = pltpu.roll(jnp.where(lane == 0, nxt, mine), LANES - 1, 1)
                total = 2.5 * mine - xm[h] - xp[h] - wl * wm - wr * wp
                for u in range(NV):
                    total = total + mix[v][u] * cur[u][h]
                if h == 0:
                    total = total + extra * mine
                out_ref[(v * 2 + h) * TILES_W + c] = mine - scale[h] * total
        return carry

    lax.fori_loop(0, TILES_W, body, 0)


def pack_kernel(state_ref, chip_ref, fall_ref, chip_out_ref, pair_out_ref):
    even = lax.axis_index("space") % 2 == 0
    for v in range(NV):
        direct = fall_ref[v]
        own = chip_ref[v, 1:3] + jnp.where(even, direct, 0.0)
        chip_out_ref[v, 0:1] = chip_ref[v, 0:1]
        chip_out_ref[v, 1:3] = own
        pair_out_ref[v, 0:1] = jnp.where(even, state_ref[0, v, CX - 1 : CX], state_ref[0, v, 0:1])
        pair_out_ref[v, 1:3] = own
        pair_out_ref[v, 3:4] = jnp.where(even, 0.0, direct[1:2])


def fix_kernel(
    donor_ref, inter_ref, radius_ref, kept_ref, far_ref, chip_ref, pair_ref, out_ref
):
    p = lax.axis_index("space")
    n = lax.axis_index("inst")
    even = p % 2 == 0
    row = lax.broadcasted_iota(jnp.int32, (8, LANES), 0)
    base = 2 * (p + 8 * n - 1)
    zero = jnp.zeros((8, LANES), jnp.float32)
    table = [zero for _ in range(5)]
    for j in range(RI):
        w = inter_ref[0, j]
        first = (donor_ref[0, j, 0] - base + 2 * DONORS) % DONORS
        second = (donor_ref[0, j, 1] - base + 2 * DONORS) % DONORS
        for r in range(5):
            part = jnp.where(first == r, w, 0.0) + jnp.where(second == r, 1.0 - w, 0.0)
            table[r] = jnp.where(row == j, 2.0 * part, table[r])
    far0 = jnp.where(even, table[0], table[4])
    far1 = jnp.where(even, table[1], zero)
    pair0 = jnp.where(even, table[4], table[0])
    pair1 = jnp.where(even, zero, table[1])
    lo = jnp.where(row == 0, jnp.where(p == 0, 0.0, 1.25), 0.0)
    hi = jnp.where(row == 7, jnp.where(p == SPACE - 1, 0.0, 0.25), 0.0)
    lo_chip, lo_pair = jnp.where(even, lo, zero), jnp.where(even, zero, lo)
    hi_chip, hi_pair = jnp.where(even, zero, hi), jnp.where(even, hi, zero)
    span = 2 * TILES_W
    for v in range(NV):

        def body(c, carry):
            cols = pl.ds(pl.multiple_of(c * LANES, LANES), LANES)
            top = v * span + c
            bottom = top + TILES_W
            chip_edge = chip_ref[v, 0:1, cols] + pair_ref[v, 3:4, cols]
            pair_edge = pair_ref[v, 0:1, cols]
            fix = lo_chip * chip_edge + lo_pair * pair_edge
            fix = fix + far0 * far_ref[v, 0:1, cols] + far1 * far_ref[v, 1:2, cols]
            fix = fix + table[2] * chip_ref[v, 1:2, cols] + table[3] * chip_ref[v, 2:3, cols]
            fix = fix + pair0 * pair_ref[v, 1:2, cols] + pair1 * pair_ref[v, 2:3, cols]
            scale = 0.5 / radius_ref[0:8, cols]
            out_ref[top] = kept_ref[top] + scale * fix
            scale = 0.5 / radius_ref[8:16, cols]
            out_ref[bottom] = kept_ref[bottom] + scale * (
                hi_chip * chip_edge + hi_pair * pair_edge
            )
            return carry

        lax.fori_loop(0, TILES_W, body, 0, unroll=8)


def add_kernel(kept_ref, spec_ref, out_ref, held, sems):
    span = 2 * TILES_W
    copies = []
    for v in range(NV):

        def body(t, carry):
            held[v * span + t] = kept_ref[v * span + t] + spec_ref[v * span + t]
            return carry

        lax.fori_loop(0, span, body, 0, unroll=8)
        part = pl.ds(v * span, span)
        copies.append(pltpu.make_async_copy(held.at[part], out_ref.at[part], sems.at[v]))
        copies[-1].start()
    for copy in copies:
        copy.wait()


def on_device(state, radius, mixing, donor, intersection):
    vmem = pl.BlockSpec(memory_space=pltpu.VMEM)
    smem = pl.BlockSpec(memory_space=pltpu.SMEM)
    limit = pltpu.CompilerParams(vmem_limit_bytes=8 * 1024 * 1024)
    field = state[0]
    tiles = field.reshape(NV, 2, 8, TILES_W, LANES).transpose(0, 1, 3, 2, 4).reshape(-1, 8, LANES)
    even = lax.axis_index("space") % 2 == 0
    moves = [
        (n * SPACE + (p + 8 * n + 2 * (p % 2) - 1) % SPACE, n * SPACE + p)
        for n in range(NT)
        for p in range(SPACE)
    ]
    donors = field[:, CX - 2 :]
    direct = [(n * SPACE + (p + 8 * n) % SPACE, n * SPACE + p) for n in range(NT) for p in (0, HALF)]
    direct += [(n * SPACE + HALF - 1, n * SPACE + HALF + 1) for n in range(NT)]
    fall = lax.ppermute(donors, ("inst", "space"), direct)
    far = lax.ppermute(donors, ("inst", "space"), moves)
    spread = lax.all_to_all(tiles, "inst", 0, 0, tiled=True)

    mixed = pl.pallas_call(
        spectral_kernel,
        out_shape=jax.ShapeDtypeStruct((NT, CHUNK, 8, LANES), jnp.float32),
        in_specs=[vmem, vmem],
        out_specs=pl.BlockSpec(memory_space=pl.ANY),
        scratch_shapes=[
            pltpu.VMEM((NT, CHUNK, 8, LANES), jnp.float32),
            pltpu.SemaphoreType.DMA((PARTS,)),
        ],
        compiler_params=limit,
        cost_estimate=pl.CostEstimate(flops=3_000_000, bytes_accessed=1_700_000, transcendentals=0),
        name="spectral",
    )(spread.reshape(NT, CHUNK, 8, LANES), radius)
    spec = lax.all_to_all(mixed.reshape(-1, 8, LANES), "inst", 0, 0, tiled=True)

    far, fall = lax.optimization_barrier((far, fall))
    first, last = field[:, :1], field[:, CX - 1 :]
    chip = lax.ppermute(
        jnp.concatenate([jnp.where(even, first, last), far], axis=1),
        "space",
        [
            (p, (p + 2 * (p % 2) - 1) % SPACE)
            for p in range(SPACE)
            if p not in (HALF - 1, SPACE - 1)
        ],
    )
    kept = pl.pallas_call(
        flux_kernel,
        out_shape=jax.ShapeDtypeStruct(tiles.shape, jnp.float32),
        in_specs=[smem, vmem, vmem],
        out_specs=vmem,
        compiler_params=limit,
        cost_estimate=pl.CostEstimate(flops=6_000_000, bytes_accessed=2_000_000, transcendentals=0),
        name="flux",
    )(mixing, state, radius)
    chip, kept = lax.optimization_barrier((chip, kept))
    chip, pair_send = pl.pallas_call(
        pack_kernel,
        out_shape=[
            jax.ShapeDtypeStruct((NV, 3, CW), jnp.float32),
            jax.ShapeDtypeStruct((NV, 4, CW), jnp.float32),
        ],
        in_specs=[vmem] * 3,
        out_specs=[vmem] * 2,
        compiler_params=limit,
        cost_estimate=pl.CostEstimate(flops=100_000, bytes_accessed=800_000, transcendentals=0),
        name="pack",
    )(state, chip, fall)
    pair = lax.ppermute(pair_send, "space", [(p, p ^ 1) for p in range(SPACE)])
    fixed = pl.pallas_call(
        fix_kernel,
        out_shape=jax.ShapeDtypeStruct(tiles.shape, jnp.float32),
        in_specs=[smem, smem] + [vmem] * 5,
        out_specs=vmem,
        compiler_params=limit,
        cost_estimate=pl.CostEstimate(flops=3_000_000, bytes_accessed=2_000_000, transcendentals=0),
        name="fix",
    )(donor, intersection, radius, kept, far, chip, pair)
    fixed, spec = lax.optimization_barrier((fixed, spec))
    total = pl.pallas_call(
        add_kernel,
        out_shape=jax.ShapeDtypeStruct(tiles.shape, jnp.float32),
        in_specs=[vmem] * 2,
        out_specs=pl.BlockSpec(memory_space=pl.ANY),
        scratch_shapes=[
            pltpu.VMEM(tiles.shape, jnp.float32),
            pltpu.SemaphoreType.DMA((NV,)),
        ],
        compiler_params=limit,
        cost_estimate=pl.CostEstimate(flops=200_000, bytes_accessed=2_400_000, transcendentals=0),
        name="add",
    )(fixed, spec)
    total = total.reshape(NV, 2, TILES_W, 8, LANES).transpose(0, 1, 3, 2, 4)
    return total.reshape(state.shape)


def solution(mesh):
    in_specs = (
        P("inst", None, "space", None),
        P("space", None),
        P(),
        P("inst", "space", None),
        P("inst", "space"),
    )
    out_specs = P("inst", None, "space", None)
    return jax.shard_map(
        on_device, mesh=mesh, in_specs=in_specs, out_specs=out_specs, check_vma=False
    )
```
